32 devices in a mesh: grp: 1, dap: 16 (over z, y, x), ch: 1, sub: 2 (over core).
Axes of the slice: x: 2, y: 2, z: 4, core: 2. Of those that a mesh axis runs over, the one named last changes fastest.
Arguments:
- query_act: bfloat16 [4, 32, 256, 384], P('ch', None, ('grp', 'dap', 'sub')), may hold values from -8 to 8
- key_act: bfloat16 [4, 32, 256, 384], P('ch', None, ('grp', 'dap', 'sub')), may hold values from -6 to 6
- value_act: bfloat16 [4, 32, 256, 384], P('ch', None, ('grp', 'dap', 'sub')), may hold values from -6 to 6
- gate_act: bfloat16 [4, 32, 256, 384], P('ch', None, ('grp', 'dap', 'sub')), may hold values from -6 to 6
- grad_out: bfloat16 [4, 32, 256, 384], P('ch', None, ('grp', 'dap', 'sub')), may hold values from -6 to 6
- bias_pair: bfloat16 [4, 384, 384], P('ch', ('grp', 'dap', 'sub')), may hold values from -6 to 6
- residue_mask: int32 [384], P('grp'), may hold values 0 or 1
- chain_index: int32 [384], P('grp'), may hold values from 0 to 5, never falling along the last dimension, each value on 1 to 128 neighbouring positions
- chain_bias: float32 [4], P('ch'), may hold values from -2 to 2
Outputs:
- grad_query: bfloat16 [4, 32, 256, 384], P('ch', None, ('grp', 'dap', 'sub'))
- grad_key: bfloat16 [4, 32, 256, 384], P('ch', None, ('grp', 'dap', 'sub'))
- grad_value: bfloat16 [4, 32, 256, 384], P('ch', None, ('grp', 'dap', 'sub'))
- grad_gate: bfloat16 [4, 32, 256, 384], P('ch', None, ('grp', 'dap', 'sub'))
- grad_bias: float32 [4, 384, 384], P('ch', ('grp', 'dap', 'sub'))
The draws below stay inside these ranges and needn't reach their ends.
All inputs are finite; a program needn't handle non-finite values.
Results may differ from the reference program's by a relative error of at most 0.025.
Values may be sent and summed in bfloat16 or wider, within the bound.
A program may use at most 64 MiB of HBM per device.

```python
import math
import jax
import jax.numpy as jnp
import numpy as np
from jax import lax

H = 4
DH = 32
N = 384
R = 256


def draw_query_act(key, part):
    key = jax.random.fold_in(key, 11)
    drawn = jnp.clip(jax.random.normal(key, (H, DH, R, N), jnp.float32), -6.0, 6.0)
    return drawn.astype(jnp.bfloat16)


def draw_key_act(key, part):
    key = jax.random.fold_in(key, 23)
    drawn = jnp.clip(jax.random.normal(key, (H, DH, R, N), jnp.float32), -6.0, 6.0)
    return drawn.astype(jnp.bfloat16)


def touch_ends(values, stream_key, smallest, high):
    longest = values.shape.index(max(values.shape))
    spots = []
    for shift in (0, 1):
        where = [jax.random.randint(jax.random.fold_in(stream_key, axis), (), 0, length) for axis, length in enumerate(values.shape)]
        where[longest] = (where[longest] + shift) % values.shape[longest]
        spots.append(tuple(where))
    return values.at[spots[0]].set(smallest).at[spots[1]].set(high)


def raised(values, stream_key, source, target, blocks, factor):
    owner, partner = [(jnp.arange(values.shape[axis_at]) // (values.shape[axis_at] // blocks)).reshape([-1 if axis == axis_at else 1 for axis in range(values.ndim)]) for axis_at in (source, target)]
    chosen = jax.random.permutation(stream_key, blocks)[partner]
    strong = (owner == chosen) | (owner == (partner + blocks // 2) % blocks)
    return jnp.where(strong, factor * values, values)


def block_levels(key, shape, cuts, low, high):
    factor_of, own = 1.0, jax.random.fold_in(key, 6)
    for dim, shards_of in cuts:
        steps = jnp.exp(jax.random.uniform(jax.random.fold_in(own, dim), (shards_of,), jnp.float32, low / len(cuts), high / len(cuts)))
        factor_of = factor_of * jnp.repeat(steps, shape[dim] // shards_of).reshape([-1 if axis == dim else 1 for axis in range(len(shape))])
    return factor_of


def profile(count, total, reach, lean):
    portions = [(1 << 20) // math.isqrt(grade ** lean) + 1 for grade in range(2, count + 1)]
    spare, holding = total - reach - (count - 1), [1] * (count - 1)
    while spare > 0:
        candidates = [i for i in range(count - 1) if holding[i] < reach]
        mass, remaining = sum([portions[i] for i in candidates]), spare
        for i in candidates:
            addition = min(reach - holding[i], max(1, remaining * portions[i] // mass), spare)
            holding[i] = holding[i] + addition
            spare = spare - addition
    return np.array([reach] + holding)


def uneven_parts(stream_key, number_of, total, reach, slope):
    if number_of == 2:
        one = jax.random.randint(stream_key, (), max(1, total - reach), min(reach, total - 1) + 1)
        return jnp.stack([one, total - one])
    lengths = jnp.asarray(profile(number_of, total, reach, slope), jnp.int32)
    twos = (number_of - 1) // 2
    giver, taker = lengths[1:1 + 2 * twos:2], lengths[2:2 + 2 * twos:2]
    margin = jnp.minimum(giver - 1, reach - taker)
    passed = jax.random.randint(jax.random.fold_in(stream_key, 1), (twos,), 0, 1 << 20) % (margin + 1)
    lengths = lengths.at[1:1 + 2 * twos:2].set(giver - passed).at[2:2 + 2 * twos:2].set(taker + passed)
    return lengths[jax.random.permutation(jax.random.fold_in(stream_key, 2), number_of)]


def scatter_about(stream_key, dims, spread, most, shards=(), dtype=jnp.bfloat16):
    result = jax.random.normal(stream_key, dims, jnp.float32) * spread
    if len(shards) > 0:
        result = block_levels(stream_key, dims, shards, -0.22, 0.18) * result
    return jnp.clip(result, min=-most, max=most).astype(dtype)


def heavy_noise(key, extent, width, most, shards, heavy, held_as=jnp.bfloat16):
    values = width * jax.random.normal(key, extent, jnp.float32)
    if shards:
        values = values * block_levels(key, extent, shards, -0.22, 0.18)
    return jnp.clip(raised(values, jax.random.fold_in(key, 3), *heavy), -most, most).astype(held_as)


def setup_inputs(seed: int = 0, part: int = 0) -> dict:
    seeds = jax.random.split(jax.random.key(seed), 10)
    part_keys = jax.random.split(jax.random.fold_in(seeds[9], part), 10)
    return {
        "query_act": draw_query_act(jax.random.fold_in(jax.random.fold_in(seeds[9], part), 71), part),
        "key_act": draw_key_act(jax.random.fold_in(jax.random.fold_in(seeds[9], part), 71), part),
        "value_act": scatter_about(part_keys[2], (H, DH, R, N), 1.0, 6.0, ((2, 32),)),
        "gate_act": scatter_about(part_keys[3], (H, DH, R, N), 1.5, 6.0, ((2, 32),)),
        "grad_out": heavy_noise(part_keys[4], (H, DH, R, N), 1.0, 6.0, ((2, 32),), (2, 3, 32, 2.75)),
        "bias_pair": scatter_about(part_keys[5], (H, N, N), 1.0, 6.0, ((1, 32),)),
        "residue_mask": touch_ends((jax.random.randint(part_keys[6], (N,), 0, 10) < 9).astype(jnp.int32), jax.random.fold_in(part_keys[6], 1), 0, 1),
        "chain_index": jnp.searchsorted(jnp.cumsum(uneven_parts(part_keys[7], 6, N, N // 3, 0)), jnp.arange(N), side="right").astype(jnp.int32),
        "chain_bias": jnp.clip(jax.random.uniform(seeds[8], (H,), jnp.float32, -2.0, 2.0), -2.0, 2.0),
    }


def pair_bias(bias_pair, residue_mask, chain_index, chain_bias):
    same_chain = (chain_index[:, None] == chain_index[None, :]).astype(jnp.float32)
    key_block = jnp.where(residue_mask > 0, 0.0, -1e9).astype(jnp.float32)
    return bias_pair.astype(jnp.float32) + chain_bias.astype(jnp.float32)[:, None, None] * same_chain[None] + key_block[None, None, :]


def row_grads(full_bias, query_row, key_row, value_row, gate_row, cotangent):
    score_scale = query_row.shape[1] ** -0.5
    query_wide = query_row.astype(jnp.float32)
    key_wide = key_row.astype(jnp.float32)
    value_wide = value_row.astype(jnp.float32)
    scores = jnp.einsum('hdj,hdk->hjk', query_wide, key_wide) * score_scale + full_bias
    attn_probs = jax.nn.softmax(scores, axis=-1)
    probs_low = attn_probs.astype(jnp.bfloat16)
    attended = jnp.einsum('hjk,hdk->hdj', probs_low.astype(jnp.float32), value_wide)
    sigmoid_gate = jax.nn.sigmoid(gate_row.astype(jnp.float32))
    cotangent_wide = cotangent.astype(jnp.float32)
    grad_gate = (cotangent_wide * attended * sigmoid_gate * (1.0 - sigmoid_gate)).astype(jnp.bfloat16)
    grad_att = (cotangent_wide * sigmoid_gate).astype(jnp.bfloat16)
    grad_value = jnp.einsum('hjk,hdj->hdk', probs_low.astype(jnp.float32), grad_att.astype(jnp.float32)).astype(jnp.bfloat16)
    grad_probs = jnp.einsum('hdj,hdk->hjk', grad_att.astype(jnp.float32), value_wide)
    row_delta = jnp.sum(grad_att.astype(jnp.float32) * attended, axis=1)
    grad_scores = attn_probs * (grad_probs - row_delta[:, :, None])
    scores_low = grad_scores.astype(jnp.bfloat16).astype(jnp.float32)
    grad_query = (score_scale * jnp.einsum('hjk,hdk->hdj', scores_low, key_wide)).astype(jnp.bfloat16)
    grad_key = (score_scale * jnp.einsum('hjk,hdj->hdk', scores_low, query_wide)).astype(jnp.bfloat16)
    return grad_scores, (grad_query, grad_key, grad_value, grad_gate)


def reference(query_act, key_act, value_act, gate_act, grad_out, bias_pair, residue_mask, chain_index, chain_bias):
    full_bias = pair_bias(bias_pair, residue_mask, chain_index, chain_bias)

    def row_step(running, row_inputs):
        grad_scores, grads = row_grads(full_bias, *row_inputs)
        return running + grad_scores, grads

    stacked = tuple(jnp.moveaxis(member, 2, 0) for member in (query_act, key_act, value_act, gate_act, grad_out))
    grad_bias, grads = lax.scan(row_step, jnp.zeros(full_bias.shape, jnp.float32), stacked)
    grad_query, grad_key, grad_value, grad_gate = (jnp.moveaxis(member, 0, 2) for member in grads)
    return grad_query, grad_key, grad_value, grad_gate, grad_bias
```

```python
import functools

import jax
import jax.numpy as jnp
from jax import lax
from jax.experimental import pallas as pl
from jax.experimental.pallas import tpu as pltpu
from jax.sharding import PartitionSpec as P

F32 = jnp.float32
BF16 = jnp.bfloat16
MESH = pl.DeviceIdType.MESH
LANES = 128
PAD = 16


def dot(a, b, ca, cb):
    return lax.dot_general(a, b, (((ca,), (cb,)), ((), ())), preferred_element_type=F32)


def kernel(
    n_dap,
    q_ref,
    k_ref,
    v_ref,
    g_ref,
    go_ref,
    bias_ref,
    mask_ref,
    chain_col,
    chain_row,
    cb_ref,
    dq_ref,
    dk_ref,
    dv_ref,
    dg_ref,
    db_ref,
    qs,
    ks,
    vs,
    gas,
    gfs,
    oq,
    ok,
    ov,
    og,
    bias_t,
    acc,
    place,
    fixed,
    same,
    gath,
    snd,
    ra,
    sb,
    rb,
    g_send,
    g_recv,
    gf_send,
    gf_recv,
    a_send,
    a_recv,
    b_send,
    b_recv,
):
    heads, dh, rows, n = q_ref.shape
    own = db_ref.shape[1]
    scale = dh ** (-0.5)
    me = lax.axis_index("dap")
    core = lax.axis_index("sub")
    other = 1 - core

    def peer_of(t):
        return lax.rem(me + t, n_dap)

    barrier = pltpu.get_barrier_semaphore()

    def greet(t, carry):
        pl.semaphore_signal(barrier, inc=1, device_id={"dap": peer_of(t)}, device_id_type=MESH)
        return carry

    lax.fori_loop(1, n_dap, greet, 0)
    pl.semaphore_signal(barrier, inc=1, device_id={"sub": other}, device_id_type=MESH)

    def gather_copy(h, t):
        return pltpu.make_async_remote_copy(
            src_ref=bias_ref.at[h],
            dst_ref=gath.at[h, core, me],
            send_sem=g_send.at[h, t],
            recv_sem=g_recv.at[h, t],
            device_id={"dap": peer_of(t)},
            device_id_type=MESH,
        )

    def forward_copy(h):
        return pltpu.make_async_remote_copy(
            src_ref=gath.at[h, core],
            dst_ref=gath.at[h, core],
            send_sem=gf_send.at[h],
            recv_sem=gf_recv.at[h],
            device_id={"sub": other},
            device_id_type=MESH,
        )

    def core_copy(h):
        return pltpu.make_async_remote_copy(
            src_ref=snd.at[h, other],
            dst_ref=ra.at[h],
            send_sem=a_send.at[h],
            recv_sem=a_recv.at[h],
            device_id={"sub": other},
            device_id_type=MESH,
        )

    def owner_copy(h, t):
        return pltpu.make_async_remote_copy(
            src_ref=sb.at[h, peer_of(t)],
            dst_ref=rb.at[h, me],
            send_sem=b_send.at[h, t],
            recv_sem=b_recv.at[h, t],
            device_id={"dap": peer_of(t)},
            device_id_type=MESH,
        )

    def each_peer(h, make, what):
        def step(t, carry):
            what(make(h, t))
            return carry

        lax.fori_loop(1, n_dap, step, 0)

    pl.semaphore_wait(barrier, n_dap)
    for h in range(heads):
        each_peer(h, gather_copy, lambda c: c.start())
    for h in range(heads):
        gath[h, core, me] = bias_ref[h]

    def forward(h):
        each_peer(h, gather_copy, lambda c: c.wait_recv())
        forward_copy(h).start()

    def reduce_owner(h):
        core_copy(h).wait_recv()
        sb[h] = (snd[h, core].astype(F32) + ra[h].astype(F32)).astype(BF16)
        rb[h, me] = sb[h, me]
        each_peer(h, owner_copy, lambda c: c.start())

    total = 2 * n_dap * PAD
    r = lax.broadcasted_iota(jnp.int32, (total, n), 0)
    j = lax.broadcasted_iota(jnp.int32, (total, n), 1)
    half = jnp.where(r >= n_dap * PAD, 1, 0)
    slot = (r - half * (n_dap * PAD)) // PAD
    inner = r % PAD
    hit = (inner < own) & ((slot * 2 + half) * own + inner == j)
    place[...] = jnp.where(hit, 1.0, 0.0).astype(BF16)

    same[...] = jnp.where(chain_col[...] == chain_row[...], 1.0, 0.0)
    fixed[...] = jnp.where(mask_ref[...] > 0, 0.0, -1000000000.0).astype(F32)

    columns = n // LANES

    def flat(x):
        return x.astype(F32).reshape(dh * rows, n)

    def put(ref, x):
        for c in range(columns):
            ref[c] = x[:, c * LANES : (c + 1) * LANES]

    def take_row(ref, i):
        at = pl.ds(i, dh, stride=rows)
        return jnp.concatenate([ref[c, at, :] for c in range(columns)], axis=1)

    def put_row(ref, i, x):
        at = pl.ds(i, dh, stride=rows)
        for c in range(columns):
            ref[c, at, :] = x[:, c * LANES : (c + 1) * LANES]

    def prepare(h):
        put(qs, flat(q_ref[h]))
        put(ks, flat(k_ref[h]))
        put(vs, flat(v_ref[h]))
        gate = 1.0 / (1.0 + jnp.exp(-flat(g_ref[h])))
        cot = flat(go_ref[h])
        att = cot * gate
        put(gas, att)
        put(gfs, att * (1.0 - gate))

    def row(i):
        q = take_row(qs, i).astype(BF16)
        k = take_row(ks, i).astype(BF16)
        v = take_row(vs, i).astype(BF16)
        ga = take_row(gas, i).astype(BF16)
        s = dot(k, q, 0, 0) * scale + bias_t[...]
        e = jnp.exp(s - jnp.max(s, axis=0, keepdims=True))
        p = e * (1.0 / jnp.sum(e, axis=0, keepdims=True))
        low = p.astype(BF16)
        attended = dot(v, low, 1, 0)
        put_row(og, i, take_row(gfs, i) * attended)
        delta = jnp.sum(ga.astype(F32) * attended, axis=0, keepdims=True)
        put_row(ov, i, dot(ga, low, 1, 1))
        ds = p * (dot(v, ga, 0, 0) - delta)
        acc[...] += ds
        dlow = ds.astype(BF16)
        put_row(oq, i, dot(k, dlow, 1, 0) * scale)
        put_row(ok, i, dot(q, dlow, 1, 1) * scale)

    def some_rows(lo, hi):
        def step(i, carry):
            row(i)
            return carry

        lax.fori_loop(lo, hi, step, 0)

    early = rows // 2
    for h in range(heads):
        prepare(h)
        acc[...] = jnp.zeros_like(acc)
        if h == 0:
            forward(0)
        forward_copy(h).wait_recv()
        moved = dot(gath[h].reshape(total, n), place[...], 0, 0)
        bias_t[...] = moved + cb_ref[h] * same[...] + fixed[...]
        some_rows(0, early)
        if h + 1 < heads:
            forward(h + 1)
        if h > 0:
            reduce_owner(h - 1)
        some_rows(early, rows)
        out = dot(place[...], acc[...].astype(BF16), 1, 1)
        snd[h] = out.astype(BF16).reshape(2, n_dap, PAD, n)
        core_copy(h).start()

        for ref, held in ((dq_ref, oq), (dk_ref, ok), (dv_ref, ov), (dg_ref, og)):
            for c in range(columns):
                part = held[c].reshape(dh, rows, LANES).astype(BF16)
                ref[h, :, :, c * LANES : (c + 1) * LANES] = part
    reduce_owner(heads - 1)
    for h in range(heads):
        each_peer(h, owner_copy, lambda c: c.wait_recv())
        db_ref[h] = jnp.sum(rb[h].astype(F32), axis=0)[:own]
    for h in range(heads):
        each_peer(h, gather_copy, lambda c: c.wait_send())
        forward_copy(h).wait_send()
        core_copy(h).wait_send()
        each_peer(h, owner_copy, lambda c: c.wait_send())


def per_device(
    n_dap,
    query_act,
    key_act,
    value_act,
    gate_act,
    grad_out,
    bias_pair,
    residue_mask,
    chain_index,
    chain_bias,
):
    heads, dh, rows, n = query_act.shape
    own = bias_pair.shape[1]
    padded = jnp.pad(bias_pair, ((0, 0), (0, PAD - own), (0, 0)))
    vmem = pl.BlockSpec(memory_space=pltpu.VMEM)
    smem = pl.BlockSpec(memory_space=pltpu.SMEM)
    dma = pltpu.SemaphoreType.DMA
    act = jax.ShapeDtypeStruct(query_act.shape, BF16)
    flat = pltpu.VMEM((n // LANES, dh * rows, LANES), F32)
    return pl.pallas_call(
        functools.partial(kernel, n_dap),
        out_shape=(act, act, act, act, jax.ShapeDtypeStruct((heads, own, n), F32)),
        in_specs=[vmem] * 9 + [smem],
        out_specs=(vmem,) * 5,
        scratch_shapes=[flat] * 9
        + [
            pltpu.VMEM((n, n), F32),
            pltpu.VMEM((n, n), F32),
            pltpu.VMEM((2 * n_dap * PAD, n), BF16),
            pltpu.VMEM((n, 1), F32),
            pltpu.VMEM((n, n), F32),
            pltpu.VMEM((heads, 2, n_dap, PAD, n), BF16),
            pltpu.VMEM((heads, 2, n_dap, PAD, n), BF16),
            pltpu.VMEM((heads, n_dap, PAD, n), BF16),
            pltpu.VMEM((heads, n_dap, PAD, n), BF16),
            pltpu.VMEM((heads, n_dap, PAD, n), BF16),
            dma((heads, n_dap)),
            dma((heads, n_dap)),
            dma((heads,)),
            dma((heads,)),
            dma((heads,)),
            dma((heads,)),
            dma((heads, n_dap)),
            dma((heads, n_dap)),
        ],
        compiler_params=pltpu.CompilerParams(
            collective_id=0, has_side_effects=True, vmem_limit_bytes=56 * 2**20
        ),
        name="triangle_grads",
    )(
        query_act,
        key_act,
        value_act,
        gate_act,
        grad_out,
        padded,
        residue_mask[:, None],
        chain_index[:, None],
        chain_index[None, :],
        chain_bias,
    )


def solution(mesh):
    slab = P("ch", None, ("grp", "dap", "sub"), None)
    pair = P("ch", ("grp", "dap", "sub"), None)
    return jax.shard_map(
        functools.partial(per_device, mesh.shape["dap"]),
        mesh=mesh,
        in_specs=(slab,) * 5 + (pair, P("grp"), P("grp"), P("ch")),
        out_specs=(slab,) * 4 + (pair,),
        check_vma=False,
    )
```

```python
import functools

import jax
import jax.numpy as jnp
from jax import lax
from jax.experimental import pallas as pl
from jax.experimental.pallas import tpu as pltpu
from jax.sharding import PartitionSpec as P

F32 = jnp.float32
BF16 = jnp.bfloat16
MESH = pl.DeviceIdType.MESH
LANES = 128
INNER = 4
PAD = 16


def dot(a, b, ca, cb):
    return lax.dot_general(a, b, (((ca,), (cb,)), ((), ())), preferred_element_type=F32)


def kernel(
    n_dap,
    q_hbm,
    k_hbm,
    v_hbm,
    g_hbm,
    go_hbm,
    rows_ref,
    mask_ref,
    chain_ref,
    cb_ref,
    dq_hbm,
    dk_hbm,
    dv_hbm,
    dg_hbm,
    db_ref,
    q_ref,
    k_ref,
    v_ref,
    g_ref,
    go_ref,
    dq_ref,
    dk_ref,
    dv_ref,
    dg_ref,
    bias_ref,
    qs,
    ks,
    vs,
    gas,
    gfs,
    oq,
    ok,
    ov,
    og,
    bias_t,
    acc,
    place,
    fixed,
    same,
    gath,
    snd,
    ra,
    sb,
    rb,
    sc,
    rc,
    in_sem,
    out_sem,
    g_send,
    g_recv,
    gi_send,
    gi_recv,
    gf_send,
    gf_recv,
    a_send,
    a_recv,
    b_send,
    b_recv,
    c_send,
    c_recv,
):
    heads, dh, rows, n = q_ref.shape
    own = db_ref.shape[0]
    scale = dh ** (-0.5)
    outer = n_dap // INNER
    me = lax.axis_index("dap")
    core = lax.axis_index("sub")
    other = 1 - core
    my_out = me // INNER
    my_in = lax.rem(me, INNER)

    moved_in = [
        pltpu.make_async_copy(src, dst, in_sem.at[x])
        for x, (src, dst) in enumerate(
            ((q_hbm, q_ref), (k_hbm, k_ref), (v_hbm, v_ref), (g_hbm, g_ref), (go_hbm, go_ref))
        )
    ]
    for copy in moved_in:
        copy.start()

    def out_of(t):
        return lax.rem(my_out + t, outer)

    def in_of(t):
        return lax.rem(my_in + t, INNER)

    def on_line(t):
        return {"dap": out_of(t) * INNER + my_in}

    def on_plane(t):
        return {"dap": my_out * INNER + in_of(t)}

    barrier = pltpu.get_barrier_semaphore()

    def greet(where):
        pl.semaphore_signal(barrier, inc=1, device_id=where, device_id_type=MESH)

    for t in range(1, outer):
        greet(on_line(t))
    for t in range(1, INNER):
        greet(on_plane(t))
    greet({"sub": other})

    def remote(src, dst, send, recv, where):
        return pltpu.make_async_remote_copy(
            src_ref=src,
            dst_ref=dst,
            send_sem=send,
            recv_sem=recv,
            device_id=where,
            device_id_type=MESH,
        )

    def line_copy(h, t):
        dst = gath.at[h, core, my_in, my_out]
        return remote(bias_ref.at[h], dst, g_send.at[h, t], g_recv.at[h, t], on_line(t))

    def plane_copy(h, t):
        held = gath.at[h, core, my_in]
        return remote(held, held, gi_send.at[h, t], gi_recv.at[h, t], on_plane(t))

    def forward_copy(h):
        held = gath.at[h, core]
        return remote(held, held, gf_send.at[h], gf_recv.at[h], {"sub": other})

    def core_copy(h):
        return remote(snd.at[h, other], ra.at[h], a_send.at[h], a_recv.at[h], {"sub": other})

    def plane_sum_copy(h, t):
        src, dst = sb.at[h, in_of(t)], rb.at[h, my_in]
        return remote(src, dst, b_send.at[h, t], b_recv.at[h, t], on_plane(t))

    def line_sum_copy(h, t):
        src, dst = sc.at[h, out_of(t)], rc.at[h, my_out]
        return remote(src, dst, c_send.at[h, t], c_recv.at[h, t], on_line(t))

    def lines(h, make, what):
        for t in range(1, outer):
            what(make(h, t))

    def planes(h, make, what):
        for t in range(1, INNER):
            what(make(h, t))

    def start(c):
        c.start()

    def arrive(c):
        c.wait_recv()

    def left(c):
        c.wait_send()

    mine = rows_ref[...].astype(F32)
    for h in range(heads):
        block = jnp.concatenate([mine[:, h, :], jnp.zeros((PAD - own, n), F32)], axis=0)
        bias_ref[h] = block.astype(BF16)

    pl.semaphore_wait(barrier, outer + INNER - 1)
    for h in range(heads):
        lines(h, line_copy, start)
    for h in range(heads):
        gath[h, core, my_in, my_out] = bias_ref[h]

    def to_plane(h):
        lines(h, line_copy, arrive)
        planes(h, plane_copy, start)

    def to_core(h):
        planes(h, plane_copy, arrive)
        forward_copy(h).start()

    def sum_cores(h):
        core_copy(h).wait_recv()
        sb[h] = (snd[h, core].astype(F32) + ra[h].astype(F32)).astype(BF16)
        rb[h, my_in] = sb[h, my_in]
        planes(h, plane_sum_copy, start)

    def sum_plane(h):
        planes(h, plane_sum_copy, arrive)
        sc[h] = jnp.sum(rb[h].astype(F32), axis=0).astype(BF16)
        rc[h, my_out] = sc[h, my_out]
        lines(h, line_sum_copy, start)

    def sum_line(h):
        lines(h, line_sum_copy, arrive)
        db_ref[:, h, :] = jnp.sum(rc[h].astype(F32), axis=0)[:own]

    total = 2 * n_dap * PAD
    r = lax.broadcasted_iota(jnp.int32, (total, n), 0)
    j = lax.broadcasted_iota(jnp.int32, (total, n), 1)
    half = jnp.where(r >= n_dap * PAD, 1, 0)
    held = (r - half * (n_dap * PAD)) // PAD
    inner = r % PAD
    slot = (held % outer) * INNER + held // outer
    hit = (inner < own) & ((slot * 2 + half) * own + inner == j)
    place[...] = jnp.where(hit, 1.0, 0.0).astype(BF16)

    def wide(x):
        return jnp.broadcast_to(x.reshape(1, n), (8, n))

    chain = wide(chain_ref[...].astype(F32))
    same[...] = jnp.where(chain.T[:, :1] == chain[:1], 1.0, 0.0)
    blocked = wide(jnp.where(mask_ref[...] > 0, 0.0, -1000000000.0).astype(F32))
    fixed[...] = blocked.T[:, :1]

    columns = n // LANES

    def flat(x):
        return x.astype(F32).reshape(dh * rows, n)

    def put(ref, x):
        for c in range(columns):
            ref[c] = x[:, c * LANES : (c + 1) * LANES]

    def take_row(ref, i):
        at = pl.ds(i, dh, stride=rows)
        return jnp.concatenate([ref[c, at, :] for c in range(columns)], axis=1)

    def put_row(ref, i, x):
        at = pl.ds(i, dh, stride=rows)
        for c in range(columns):
            ref[c, at, :] = x[:, c * LANES : (c + 1) * LANES]

    def prepare(h):
        put(qs, flat(q_ref[h]))
        put(ks, flat(k_ref[h]))
        put(vs, flat(v_ref[h]))
        gate = 1.0 / (1.0 + jnp.exp(-flat(g_ref[h])))
        cot = flat(go_ref[h])
        att = cot * gate
        put(gas, att)
        put(gfs, att * (1.0 - gate))

    def row(i):
        q = take_row(qs, i).astype(BF16)
        k = take_row(ks, i).astype(BF16)
        v = take_row(vs, i).astype(BF16)
        ga = take_row(gas, i).astype(BF16)
        s = dot(k, q, 0, 0) * scale + bias_t[...]
        e = jnp.exp(s - jnp.max(s, axis=0, keepdims=True))
        p = e * (1.0 / jnp.sum(e, axis=0, keepdims=True))
        low = p.astype(BF16)
        attended = dot(v, low, 1, 0)
        put_row(og, i, take_row(gfs, i) * attended)
        delta = jnp.sum(ga.astype(F32) * attended, axis=0, keepdims=True)
        put_row(ov, i, dot(ga, low, 1, 1))
        ds = p * (dot(v, ga, 0, 0) - delta)
        acc[...] += ds
        dlow = ds.astype(BF16)
        put_row(oq, i, dot(k, dlow, 1, 0) * scale)
        put_row(ok, i, dot(q, dlow, 1, 1) * scale)

    def some_rows(lo, hi):
        def step(i, carry):
            row(i)
            return carry

        lax.fori_loop(lo, hi, step, 0)

    outs = [(dq_ref, oq, dq_hbm), (dk_ref, ok, dk_hbm), (dv_ref, ov, dv_hbm), (dg_ref, og, dg_hbm)]

    def out_copy(h, x):
        return pltpu.make_async_copy(outs[x][0].at[h], outs[x][2].at[h], out_sem.at[h, x])

    to_plane(0)
    for copy in moved_in:
        copy.wait()
    for h in range(heads):
        prepare(h)
        acc[...] = jnp.zeros_like(acc)
        if h == 0:
            to_core(0)
        forward_copy(h).wait_recv()
        moved = dot(gath[h].reshape(total, n), place[...], 0, 0)
        bias_t[...] = moved + cb_ref[h] * same[...] + fixed[...]
        some_rows(0, rows // 4)
        if h + 1 < heads:
            to_plane(h + 1)
        if h > 0:
            sum_cores(h - 1)
        some_rows(rows // 4, rows * 5 // 8)
        if h + 1 < heads:
            to_core(h + 1)
        if h > 0:
            sum_plane(h - 1)
        some_rows(rows * 5 // 8, rows)
        if h > 0:
            sum_line(h - 1)
        out = dot(place[...], acc[...].astype(BF16), 1, 1)
        snd[h] = out.astype(BF16).reshape(2, INNER, outer, PAD, n)
        core_copy(h).start()
        for x, (ref, held, _) in enumerate(outs):
            for c in range(columns):
                part = held[c].reshape(dh, rows, LANES).astype(BF16)
                ref[h, :, :, c * LANES : (c + 1) * LANES] = part
            out_copy(h, x).start()
    sum_cores(heads - 1)
    sum_plane(heads - 1)
    sum_line(heads - 1)
    for h in range(heads):
        for x in range(4):
            out_copy(h, x).wait()
        lines(h, line_copy, left)
        planes(h, plane_copy, left)
        forward_copy(h).wait_send()
        core_copy(h).wait_send()
        planes(h, plane_sum_copy, left)
        lines(h, line_sum_copy, left)


def per_device(
    n_dap,
    query_act,
    key_act,
    value_act,
    gate_act,
    grad_out,
    bias_pair,
    residue_mask,
    chain_index,
    chain_bias,
):
    heads, dh, rows, n = query_act.shape
    own = bias_pair.shape[1]
    outer = n_dap // INNER
    vmem = pl.BlockSpec(memory_space=pltpu.VMEM)
    smem = pl.BlockSpec(memory_space=pltpu.SMEM)
    hbm = pl.BlockSpec(memory_space=pl.ANY)
    dma = pltpu.SemaphoreType.DMA
    act = jax.ShapeDtypeStruct(query_act.shape, BF16)
    flat = pltpu.VMEM((n // LANES, dh * rows, LANES), F32)
    *grads, grad_bias = pl.pallas_call(
        functools.partial(kernel, n_dap),
        out_shape=(act, act, act, act, jax.ShapeDtypeStruct((own, heads, n), F32)),
        in_specs=[hbm] * 5 + [vmem] * 3 + [smem],
        out_specs=(hbm,) * 4 + (vmem,),
        scratch_shapes=[pltpu.VMEM(query_act.shape, BF16)] * 9
        + [pltpu.VMEM((heads, PAD, n), BF16)]
        + [flat] * 9
        + [
            pltpu.VMEM((n, n), F32),
            pltpu.VMEM((n, n), F32),
            pltpu.VMEM((2 * n_dap * PAD, n), BF16),
            pltpu.VMEM((n, 1), F32),
            pltpu.VMEM((n, n), F32),
            pltpu.VMEM((heads, 2, INNER, outer, PAD, n), BF16),
            pltpu.VMEM((heads, 2, INNER, outer, PAD, n), BF16),
            pltpu.VMEM((heads, INNER, outer, PAD, n), BF16),
            pltpu.VMEM((heads, INNER, outer, PAD, n), BF16),
            pltpu.VMEM((heads, INNER, outer, PAD, n), BF16),
            pltpu.VMEM((heads, outer, PAD, n), BF16),
            pltpu.VMEM((heads, outer, PAD, n), BF16),
            dma((5,)),
            dma((heads, 4)),
            dma((heads, outer)),
            dma((heads, outer)),
            dma((heads, INNER)),
            dma((heads, INNER)),
            dma((heads,)),
            dma((heads,)),
            dma((heads,)),
            dma((heads,)),
            dma((heads, INNER)),
            dma((heads, INNER)),
            dma((heads, outer)),
            dma((heads, outer)),
        ],
        compiler_params=pltpu.CompilerParams(
            collective_id=0, has_side_effects=True, vmem_limit_bytes=56 * 2**20
        ),
        name="triangle_grads",
    )(
        query_act,
        key_act,
        value_act,
        gate_act,
        grad_out,
        jnp.swapaxes(bias_pair, 0, 1),
        residue_mask,
        chain_index,
        chain_bias,
    )
    return (*grads, jnp.swapaxes(grad_bias, 0, 1))


def solution(mesh):
    slab = P("ch", None, ("grp", "dap", "sub"), None)
    pair = P("ch", ("grp", "dap", "sub"), None)
    return jax.shard_map(
        functools.partial(per_device, mesh.shape["dap"]),
        mesh=mesh,
        in_specs=(slab,) * 5 + (pair, P("grp"), P("grp"), P("ch")),
        out_specs=(slab,) * 4 + (pair,),
        check_vma=False,
    )
```

```python
import functools

import jax
import jax.numpy as jnp
from jax import lax
from jax.experimental import pallas as pl
from jax.experimental.pallas import tpu as pltpu
from jax.sharding import PartitionSpec as P

F32 = jnp.float32
BF16 = jnp.bfloat16
MESH = pl.DeviceIdType.MESH
LANES = 128
PARTS = 2
PAD = 16


def dot(a, b, ca, cb):
    return lax.dot_general(a, b, (((ca,), (cb,)), ((), ())), preferred_element_type=F32)


def kernel(
    n_dap,
    q_hbm,
    k_hbm,
    v_hbm,
    g_hbm,
    go_hbm,
    rows_ref,
    mask_ref,
    chain_ref,
    cb_ref,
    dq_hbm,
    dk_hbm,
    dv_hbm,
    dg_hbm,
    db_ref,
    q_ref,
    k_ref,
    v_ref,
    g_ref,
    go_ref,
    dq_ref,
    dk_ref,
    dv_ref,
    dg_ref,
    bias_ref,
    qs,
    ks,
    vs,
    gas,
    gfs,
    oq,
    ok,
    ov,
    og,
    bias_t,
    acc,
    place,
    fixed,
    same,
    gath,
    snd,
    ra,
    sb,
    rb,
    in_sem,
    out_sem,
    g_send,
    g_recv,
    gf_send,
    gf_recv,
    a_send,
    a_recv,
    b_send,
    b_recv,
):
    heads, dh, rows, n = q_ref.shape
    own = db_ref.shape[0]
    scale = dh ** (-0.5)
    me = lax.axis_index("dap")
    core = lax.axis_index("sub")
    other = 1 - core

    moved_in = [
        pltpu.make_async_copy(src, dst, in_sem.at[x])
        for x, (src, dst) in enumerate(
            ((q_hbm, q_ref), (k_hbm, k_ref), (v_hbm, v_ref), (g_hbm, g_ref), (go_hbm, go_ref))
        )
    ]
    for copy in moved_in:
        copy.start()

    def peer(t):
        return lax.rem(me + t, n_dap)

    barrier = pltpu.get_barrier_semaphore()

    def greet(t, carry):
        pl.semaphore_signal(barrier, inc=1, device_id={"dap": peer(t)}, device_id_type=MESH)
        return carry

    lax.fori_loop(1, n_dap, greet, 0)
    pl.semaphore_signal(barrier, inc=1, device_id={"sub": other}, device_id_type=MESH)

    def remote(src, dst, send, recv, where):
        return pltpu.make_async_remote_copy(
            src_ref=src,
            dst_ref=dst,
            send_sem=send,
            recv_sem=recv,
            device_id=where,
            device_id_type=MESH,
        )

    def gather_copy(h, t):
        dst = gath.at[h, core, me]
        return remote(bias_ref.at[h], dst, g_send.at[h, t], g_recv.at[h, t], {"dap": peer(t)})

    def forward_copy(h):
        held = gath.at[h, core]
        return remote(held, held, gf_send.at[h], gf_recv.at[h], {"sub": other})

    def core_copy(h):
        return remote(snd.at[h, other], ra.at[h], a_send.at[h], a_recv.at[h], {"sub": other})

    def owner_copy(h, t):
        src, dst = sb.at[h, peer(t)], rb.at[h, me]
        return remote(src, dst, b_send.at[h, t], b_recv.at[h, t], {"dap": peer(t)})

    def peers(h, make, what):
        def step(t, carry):
            what(make(h, t))
            return carry

        lax.fori_loop(1, n_dap, step, 0)

    def start(c):
        c.start()

    def arrive(c):
        c.wait_recv()

    def left(c):
        c.wait_send()

    mine = rows_ref[...].astype(F32)
    for h in range(heads):
        block = jnp.concatenate([mine[:, h, :], jnp.zeros((PAD - own, n), F32)], axis=0)
        bias_ref[h] = block.astype(BF16)

    pl.semaphore_wait(barrier, n_dap)
    peers(0, gather_copy, start)
    for h in range(heads):
        gath[h, core, me] = bias_ref[h]

    def forward(h):
        peers(h, gather_copy, arrive)
        forward_copy(h).start()
        if h + 1 < heads:
            peers(h + 1, gather_copy, start)

    def sum_cores(h):
        core_copy(h).wait_recv()
        sb[h] = (snd[h, core].astype(F32) + ra[h].astype(F32)).astype(BF16)
        rb[h, me] = sb[h, me]
        peers(h, owner_copy, start)

    def sum_owner(h):
        peers(h, owner_copy, arrive)
        db_ref[:, h, :] = jnp.sum(rb[h].astype(F32), axis=0)[:own]

    total = 2 * n_dap * PAD
    r = lax.broadcasted_iota(jnp.int32, (total, n), 0)
    j = lax.broadcasted_iota(jnp.int32, (total, n), 1)
    half = jnp.where(r >= n_dap * PAD, 1, 0)
    slot = (r - half * (n_dap * PAD)) // PAD
    inner = r % PAD
    hit = (inner < own) & ((slot * 2 + half) * own + inner == j)
    place[...] = jnp.where(hit, 1.0, 0.0).astype(BF16)

    def wide(x):
        return jnp.broadcast_to(x.reshape(1, n), (8, n))

    chain = wide(chain_ref[...].astype(F32))
    same[...] = jnp.where(chain.T[:, :1] == chain[:1], 1.0, 0.0)
    blocked = wide(jnp.where(mask_ref[...] > 0, 0.0, -1000000000.0).astype(F32))
    fixed[...] = blocked.T[:, :1]

    columns = n // LANES

    def flat(x):
        return x.astype(F32).reshape(dh * rows, n)

    def put(ref, x):
        for c in range(columns):
            ref[c] = x[:, c * LANES : (c + 1) * LANES]

    def take_row(ref, i):
        at = pl.ds(i, dh, stride=rows)
        return jnp.concatenate([ref[c, at, :] for c in range(columns)], axis=1)

    def put_row(ref, i, x):
        at = pl.ds(i, dh, stride=rows)
        for c in range(columns):
            ref[c, at, :] = x[:, c * LANES : (c + 1) * LANES]

    def prepare(h):
        put(qs, flat(q_ref[h]))
        put(ks, flat(k_ref[h]))
        put(vs, flat(v_ref[h]))
        gate = 1.0 / (1.0 + jnp.exp(-flat(g_ref[h])))
        cot = flat(go_ref[h])
        att = cot * gate
        put(gas, att)
        put(gfs, att * (1.0 - gate))

    def row(i):
        q = take_row(qs, i).astype(BF16)
        k = take_row(ks, i).astype(BF16)
        v = take_row(vs, i).astype(BF16)
        ga = take_row(gas, i).astype(BF16)
        s = dot(k, q, 0, 0) * scale + bias_t[...]
        e = jnp.exp(s - jnp.max(s, axis=0, keepdims=True))
        p = e * (1.0 / jnp.sum(e, axis=0, keepdims=True))
        low = p.astype(BF16)
        attended = dot(v, low, 1, 0)
        put_row(og, i, take_row(gfs, i) * attended)
        delta = jnp.sum(ga.astype(F32) * attended, axis=0, keepdims=True)
        put_row(ov, i, dot(ga, low, 1, 1))
        ds = p * (dot(v, ga, 0, 0) - delta)
        acc[...] += ds
        dlow = ds.astype(BF16)
        put_row(oq, i, dot(k, dlow, 1, 0) * scale)
        put_row(ok, i, dot(q, dlow, 1, 1) * scale)

    def some_rows(lo, hi):
        def step(i, carry):
            row(2 * i)
            row(2 * i + 1)
            return carry

        lax.fori_loop(lo // 2, hi // 2, step, 0)

    outs = [(dq_ref, oq, dq_hbm), (dk_ref, ok, dk_hbm), (dv_ref, ov, dv_hbm), (dg_ref, og, dg_hbm)]

    def out_copy(h, x):
        return pltpu.make_async_copy(outs[x][0].at[h], outs[x][2].at[h], out_sem.at[h, x])

    for copy in moved_in:
        copy.wait()
    early = rows // 4 * 2
    for h in range(heads):
        prepare(h)
        acc[...] = jnp.zeros_like(acc)
        if h == 0:
            forward(0)
        forward_copy(h).wait_recv()
        moved = dot(gath[h].reshape(total, n), place[...], 0, 0)
        bias_t[...] = moved + cb_ref[h] * same[...] + fixed[...]
        some_rows(0, early)
        if h + 1 < heads:
            forward(h + 1)
        if h > 0:
            sum_cores(h - 1)
        some_rows(early, rows)
        out = dot(place[...], acc[...].astype(BF16), 1, 1)
        snd[h] = out.astype(BF16).reshape(2, n_dap, PAD, n)
        core_copy(h).start()
        for x, (ref, held, _) in enumerate(outs):
            for c in range(columns):
                part = held[c].reshape(dh, rows, LANES).astype(BF16)
                ref[h, :, :, c * LANES : (c + 1) * LANES] = part
            out_copy(h, x).start()
    sum_cores(heads - 1)
    for h in range(heads):
        sum_owner(h)
    for h in range(heads):
        for x in range(4):
            out_copy(h, x).wait()
        peers(h, gather_copy, left)
        forward_copy(h).wait_send()
        core_copy(h).wait_send()
        peers(h, owner_copy, left)


def place_results(*refs):
    sources, results, held = refs[:5], refs[5:10], refs[10:15]
    in_sem, out_sem = refs[15:]
    pieces = []
    for x in range(5):
        parts = PARTS if x < 4 else 1
        for part in range(parts):
            if x < 4:
                depth = held[x].shape[1] // PARTS
                at = (slice(None), pl.ds(part * depth, depth))
            else:
                at = (slice(None),)
            mine = held[x].at[at]
            fetch = pltpu.make_async_copy(sources[x].at[at], mine, in_sem.at[x, part])
            store = pltpu.make_async_copy(mine, results[x].at[at], out_sem.at[x, part])
            pieces.append((fetch, store))
    for fetch, _ in pieces:
        fetch.start()
    for fetch, store in pieces:
        fetch.wait()
        store.start()
    for _, store in pieces:
        store.wait()


def per_device(
    n_dap,
    query_act,
    key_act,
    value_act,
    gate_act,
    grad_out,
    bias_pair,
    residue_mask,
    chain_index,
    chain_bias,
):
    heads, dh, rows, n = query_act.shape
    own = bias_pair.shape[1]
    vmem = pl.BlockSpec(memory_space=pltpu.VMEM)
    smem = pl.BlockSpec(memory_space=pltpu.SMEM)
    hbm = pl.BlockSpec(memory_space=pl.ANY)
    dma = pltpu.SemaphoreType.DMA
    act = jax.ShapeDtypeStruct(query_act.shape, BF16)
    flat = pltpu.VMEM((n // LANES, dh * rows, LANES), F32)
    *grads, grad_bias = pl.pallas_call(
        functools.partial(kernel, n_dap),
        out_shape=(act, act, act, act, jax.ShapeDtypeStruct((own, heads, n), F32)),
        in_specs=[hbm] * 5 + [vmem] * 3 + [smem],
        out_specs=(hbm,) * 4 + (vmem,),
        scratch_shapes=[pltpu.VMEM(query_act.shape, BF16)] * 9
        + [pltpu.VMEM((heads, PAD, n), BF16)]
        + [flat] * 9
        + [
            pltpu.VMEM((n, n), F32),
            pltpu.VMEM((n, n), F32),
            pltpu.VMEM((2 * n_dap * PAD, n), BF16),
            pltpu.VMEM((n, 1), F32),
            pltpu.VMEM((n, n), F32),
            pltpu.VMEM((heads, 2, n_dap, PAD, n), BF16),
            pltpu.VMEM((heads, 2, n_dap, PAD, n), BF16),
            pltpu.VMEM((heads, n_dap, PAD, n), BF16),
            pltpu.VMEM((heads, n_dap, PAD, n), BF16),
            pltpu.VMEM((heads, n_dap, PAD, n), BF16),
            dma((5,)),
            dma((heads, 4)),
            dma((heads, n_dap)),
            dma((heads, n_dap)),
            dma((heads,)),
            dma((heads,)),
            dma((heads,)),
            dma((heads,)),
            dma((heads, n_dap)),
            dma((heads, n_dap)),
        ],
        compiler_params=pltpu.CompilerParams(
            collective_id=0, has_side_effects=True, vmem_limit_bytes=56 * 2**20
        ),
        name="triangle_grads",
    )(
        query_act,
        key_act,
        value_act,
        gate_act,
        grad_out,
        jnp.swapaxes(bias_pair, 0, 1),
        residue_mask,
        chain_index,
        chain_bias,
    )
    *grads, grad_bias = pl.pallas_call(
        place_results,
        out_shape=(act, act, act, act, jax.ShapeDtypeStruct((own, heads, n), F32)),
        in_specs=[hbm] * 5,
        out_specs=(hbm,) * 5,
        scratch_shapes=[pltpu.VMEM(query_act.shape, BF16)] * 4
        + [pltpu.VMEM((own, heads, n), F32), dma((5, PARTS)), dma((5, PARTS))],
        compiler_params=pltpu.CompilerParams(vmem_limit_bytes=60 * 2**20),
        name="place_results",
    )(*grads, grad_bias)
    return (*grads, jnp.swapaxes(grad_bias, 0, 1))


def solution(mesh):
    slab = P("ch", None, ("grp", "dap", "sub"), None)
    pair = P("ch", ("grp", "dap", "sub"), None)
    return jax.shard_map(
        functools.partial(per_device, mesh.shape["dap"]),
        mesh=mesh,
        in_specs=(slab,) * 5 + (pair, P("grp"), P("grp"), P("ch")),
        out_specs=(slab,) * 4 + (pair,),
        check_vma=False,
    )
```

```python
import functools

import jax
import jax.numpy as jnp
from jax import lax
from jax.experimental import pallas as pl
from jax.experimental.pallas import tpu as pltpu
from jax.sharding import PartitionSpec as P

F32 = jnp.float32
BF16 = jnp.bfloat16
MESH = pl.DeviceIdType.MESH
LANES = 128
PARTS = 2
PAD = 16


def dot(a, b, ca, cb):
    return lax.dot_general(a, b, (((ca,), (cb,)), ((), ())), preferred_element_type=F32)


def kernel(
    n_dap,
    q_hbm,
    k_hbm,
    v_hbm,
    g_hbm,
    go_hbm,
    rows_ref,
    mask_ref,
    chain_ref,
    cb_ref,
    dq_hbm,
    dk_hbm,
    dv_hbm,
    dg_hbm,
    db_ref,
    q_ref,
    k_ref,
    v_ref,
    g_ref,
    go_ref,
    dq_ref,
    dk_ref,
    dv_ref,
    dg_ref,
    bias_ref,
    qs,
    ks,
    vs,
    gas,
    gfs,
    oq,
    ok,
    ov,
    og,
    bias_t,
    acc,
    place,
    fixed,
    same,
    gath,
    snd,
    ra,
    sb,
    rb,
    in_sem,
    out_sem,
    g_send,
    g_recv,
    gf_send,
    gf_recv,
    a_send,
    a_recv,
    b_send,
    b_recv,
):
    heads, dh, rows, n = q_ref.shape
    own = db_ref.shape[0]
    scale = dh ** (-0.5)
    me = lax.axis_index("dap")
    core = lax.axis_index("sub")
    other = 1 - core

    moved_in = [
        pltpu.make_async_copy(src, dst, in_sem.at[x])
        for x, (src, dst) in enumerate(
            ((q_hbm, q_ref), (k_hbm, k_ref), (v_hbm, v_ref), (g_hbm, g_ref), (go_hbm, go_ref))
        )
    ]
    for copy in moved_in:
        copy.start()

    def peer(t):
        return lax.rem(me + t, n_dap)

    barrier = pltpu.get_barrier_semaphore()

    def greet(t, carry):
        pl.semaphore_signal(barrier, inc=1, device_id={"dap": peer(t)}, device_id_type=MESH)
        return carry

    lax.fori_loop(1, n_dap, greet, 0)
    pl.semaphore_signal(barrier, inc=1, device_id={"sub": other}, device_id_type=MESH)

    def remote(src, dst, send, recv, where):
        return pltpu.make_async_remote_copy(
            src_ref=src,
            dst_ref=dst,
            send_sem=send,
            recv_sem=recv,
            device_id=where,
            device_id_type=MESH,
        )

    def gather_copy(h, t):
        dst = gath.at[h, core, me]
        return remote(bias_ref.at[h], dst, g_send.at[h, t], g_recv.at[h, t], {"dap": peer(t)})

    def forward_copy(h):
        held = gath.at[h, core]
        return remote(held, held, gf_send.at[h], gf_recv.at[h], {"sub": other})

    def core_copy(h):
        return remote(snd.at[h, other], ra.at[h], a_send.at[h], a_recv.at[h], {"sub": other})

    def owner_copy(h, t):
        src, dst = sb.at[h, peer(t)], rb.at[h, me]
        return remote(src, dst, b_send.at[h, t], b_recv.at[h, t], {"dap": peer(t)})

    def peers(h, make, what):
        def step(t, carry):
            what(make(h, t))
            return carry

        lax.fori_loop(1, n_dap, step, 0)

    def start(c):
        c.start()

    def arrive(c):
        c.wait_recv()

    def left(c):
        c.wait_send()

    mine = rows_ref[...].astype(F32)
    for h in range(heads):
        block = jnp.concatenate([mine[:, h, :], jnp.zeros((PAD - own, n), F32)], axis=0)
        bias_ref[h] = block.astype(BF16)

    pl.semaphore_wait(barrier, n_dap)
    peers(0, gather_copy, start)
    for h in range(heads):
        gath[h, core, me] = bias_ref[h]

    def forward(h):
        peers(h, gather_copy, arrive)
        forward_copy(h).start()
        if h + 1 < heads:
            peers(h + 1, gather_copy, start)

    def sum_cores(h):
        core_copy(h).wait_recv()
        sb[h] = (snd[h, core].astype(F32) + ra[h].astype(F32)).astype(BF16)
        rb[h, me] = sb[h, me]
        peers(h, owner_copy, start)

    def sum_owner(h):
        peers(h, owner_copy, arrive)
        db_ref[:, h, :] = jnp.sum(rb[h].astype(F32), axis=0)[:own]

    total = 2 * n_dap * PAD
    r = lax.broadcasted_iota(jnp.int32, (total, n), 0)
    j = lax.broadcasted_iota(jnp.int32, (total, n), 1)
    half = jnp.where(r >= n_dap * PAD, 1, 0)
    slot = (r - half * (n_dap * PAD)) // PAD
    inner = r % PAD
    hit = (inner < own) & ((slot * 2 + half) * own + inner == j)
    place[...] = jnp.where(hit, 1.0, 0.0).astype(BF16)

    def wide(x):
        return jnp.broadcast_to(x.reshape(1, n), (8, n))

    chain = wide(chain_ref[...].astype(F32))
    same[...] = jnp.where(chain.T[:, :1] == chain[:1], 1.0, 0.0)
    blocked = wide(jnp.where(mask_ref[...] > 0, 0.0, -1000000000.0).astype(F32))
    fixed[...] = blocked.T[:, :1]

    columns = n // LANES

    def flat(x):
        return x.astype(F32).reshape(dh * rows, n)

    def put(ref, x):
        for c in range(columns):
            ref[c] = x[:, c * LANES : (c + 1) * LANES]

    def take_row(ref, i):
        at = pl.ds(i, dh, stride=rows)
        return jnp.concatenate([ref[c, at, :] for c in range(columns)], axis=1)

    def put_row(ref, i, x):
        at = pl.ds(i, dh, stride=rows)
        for c in range(columns):
            ref[c, at, :] = x[:, c * LANES : (c + 1) * LANES]

    def prepare(h):
        put(qs, flat(q_ref[h]))
        put(ks, flat(k_ref[h]))
        put(vs, flat(v_ref[h]))
        gate = 1.0 / (1.0 + jnp.exp(-flat(g_ref[h])))
        cot = flat(go_ref[h])
        att = cot * gate
        put(gas, att)
        put(gfs, att * (1.0 - gate))

    def row(i):
        q = take_row(qs, i).astype(BF16)
        k = take_row(ks, i).astype(BF16)
        v = take_row(vs, i).astype(BF16)
        ga = take_row(gas, i).astype(BF16)
        s = dot(k, q, 0, 0) * scale + bias_t[...]
        e = jnp.exp(s - jnp.max(s, axis=0, keepdims=True))
        p = e * (1.0 / jnp.sum(e, axis=0, keepdims=True))
        low = p.astype(BF16)
        attended = dot(v, low, 1, 0)
        put_row(og, i, take_row(gfs, i) * attended)
        delta = jnp.sum(ga.astype(F32) * attended, axis=0, keepdims=True)
        put_row(ov, i, dot(ga, low, 1, 1))
        ds = p * (dot(v, ga, 0, 0) - delta)
        acc[...] += ds
        dlow = ds.astype(BF16)
        put_row(oq, i, dot(k, dlow, 1, 0) * scale)
        put_row(ok, i, dot(q, dlow, 1, 1) * scale)

    def some_rows(lo, hi):
        def step(i, carry):
            row(2 * i)
            row(2 * i + 1)
            return carry

        lax.fori_loop(lo // 2, hi // 2, step, 0)

    outs = [(dq_ref, oq, dq_hbm), (dk_ref, ok, dk_hbm), (dv_ref, ov, dv_hbm), (dg_ref, og, dg_hbm)]

    def out_copy(h, x):
        return pltpu.make_async_copy(outs[x][0].at[h], outs[x][2].at[h], out_sem.at[h, x])

    early = rows // 4 * 2
    for h in range(heads):
        if h == 0:
            forward(0)
            for copy in moved_in:
                copy.wait()
        prepare(h)
        acc[...] = jnp.zeros_like(acc)
        forward_copy(h).wait_recv()
        moved = dot(gath[h].reshape(total, n), place[...], 0, 0)
        bias_t[...] = moved + cb_ref[h] * same[...] + fixed[...]
        some_rows(0, early)
        if h + 1 < heads:
            forward(h + 1)
        if h > 0:
            sum_cores(h - 1)
        some_rows(early, rows)
        out = dot(place[...], acc[...].astype(BF16), 1, 1)
        snd[h] = out.astype(BF16).reshape(2, n_dap, PAD, n)
        core_copy(h).start()
        for x, (ref, held, _) in enumerate(outs):
            for c in range(columns):
                part = held[c].reshape(dh, rows, LANES).astype(BF16)
                ref[h, :, :, c * LANES : (c + 1) * LANES] = part
            out_copy(h, x).start()
    sum_cores(heads - 1)
    for h in range(heads):
        sum_owner(h)
    for h in range(heads):
        for x in range(4):
            out_copy(h, x).wait()
        peers(h, gather_copy, left)
        forward_copy(h).wait_send()
        core_copy(h).wait_send()
        peers(h, owner_copy, left)


def place_results(*refs):
    sources, results, held = refs[:5], refs[5:10], refs[10:15]
    in_sem, out_sem = refs[15:]
    pieces = []
    for x in range(5):
        parts = PARTS if x < 4 else 1
        for part in range(parts):
            if x < 4:
                depth = held[x].shape[1] // PARTS
                at = (slice(None), pl.ds(part * depth, depth))
            else:
                at = (slice(None),)
            mine = held[x].at[at]
            fetch = pltpu.make_async_copy(sources[x].at[at], mine, in_sem.at[x, part])
            store = pltpu.make_async_copy(mine, results[x].at[at], out_sem.at[x, part])
            pieces.append((fetch, store))
    for fetch, _ in pieces:
        fetch.start()
    for fetch, store in pieces:
        fetch.wait()
        store.start()
    for _, store in pieces:
        store.wait()


def per_device(
    n_dap,
    query_act,
    key_act,
    value_act,
    gate_act,
    grad_out,
    bias_pair,
    residue_mask,
    chain_index,
    chain_bias,
):
    heads, dh, rows, n = query_act.shape
    own = bias_pair.shape[1]
    vmem = pl.BlockSpec(memory_space=pltpu.VMEM)
    smem = pl.BlockSpec(memory_space=pltpu.SMEM)
    hbm = pl.BlockSpec(memory_space=pl.ANY)
    dma = pltpu.SemaphoreType.DMA
    act = jax.ShapeDtypeStruct(query_act.shape, BF16)
    flat = pltpu.VMEM((n // LANES, dh * rows, LANES), F32)
    *grads, grad_bias = pl.pallas_call(
        functools.partial(kernel, n_dap),
        out_shape=(act, act, act, act, jax.ShapeDtypeStruct((own, heads, n), F32)),
        in_specs=[hbm] * 5 + [vmem] * 3 + [smem],
        out_specs=(hbm,) * 4 + (vmem,),
        scratch_shapes=[pltpu.VMEM(query_act.shape, BF16)] * 9
        + [pltpu.VMEM((heads, PAD, n), BF16)]
        + [flat] * 9
        + [
            pltpu.VMEM((n, n), F32),
            pltpu.VMEM((n, n), F32),
            pltpu.VMEM((2 * n_dap * PAD, n), BF16),
            pltpu.VMEM((n, 1), F32),
            pltpu.VMEM((n, n), F32),
            pltpu.VMEM((heads, 2, n_dap, PAD, n), BF16),
            pltpu.VMEM((heads, 2, n_dap, PAD, n), BF16),
            pltpu.VMEM((heads, n_dap, PAD, n), BF16),
            pltpu.VMEM((heads, n_dap, PAD, n), BF16),
            pltpu.VMEM((heads, n_dap, PAD, n), BF16),
            dma((5,)),
            dma((heads, 4)),
            dma((heads, n_dap)),
            dma((heads, n_dap)),
            dma((heads,)),
            dma((heads,)),
            dma((heads,)),
            dma((heads,)),
            dma((heads, n_dap)),
            dma((heads, n_dap)),
        ],
        compiler_params=pltpu.CompilerParams(
            collective_id=0, has_side_effects=True, vmem_limit_bytes=56 * 2**20
        ),
        name="triangle_grads",
    )(
        query_act,
        key_act,
        value_act,
        gate_act,
        grad_out,
        jnp.swapaxes(bias_pair, 0, 1),
        residue_mask,
        chain_index,
        chain_bias,
    )
    *grads, grad_bias = pl.pallas_call(
        place_results,
        out_shape=(act, act, act, act, jax.ShapeDtypeStruct((own, heads, n), F32)),
        in_specs=[hbm] * 5,
        out_specs=(hbm,) * 5,
        scratch_shapes=[pltpu.VMEM(query_act.shape, BF16)] * 4
        + [pltpu.VMEM((own, heads, n), F32), dma((5, PARTS)), dma((5, PARTS))],
        compiler_params=pltpu.CompilerParams(vmem_limit_bytes=60 * 2**20),
        name="place_results",
    )(*grads, grad_bias)
    return (*grads, jnp.swapaxes(grad_bias, 0, 1))


def solution(mesh):
    slab = P("ch", None, ("grp", "dap", "sub"), None)
    pair = P("ch", ("grp", "dap", "sub"), None)
    return jax.shard_map(
        functools.partial(per_device, mesh.shape["dap"]),
        mesh=mesh,
        in_specs=(slab,) * 5 + (pair, P("grp"), P("grp"), P("ch")),
        out_specs=(slab,) * 4 + (pair,),
        check_vma=False,
    )
```
